32 devices in a mesh: grp: 2 (over x), ex: 16 (over z, y, core).
Axes of the slice: x: 2, y: 2, z: 4, core: 2. Of those that a mesh axis runs over, the one named last changes fastest.
Arguments:
- train_features: bfloat16 [2, 20480, 4096], P(None, ('grp', 'ex')), parts along dimension 1, may hold values from -400 to 400
- test_features: bfloat16 [2, 256, 4096], P(None, ('grp', 'ex')), parts along dimension 1, may hold values from -64 to 64
Outputs:
- influence: bfloat16 [20480, 128], P(('grp', 'ex')), parts along dimension 0
The draws below stay inside these ranges and needn't reach their ends.
There are 2 independent parts, one for each index of `grp`. The reference program is written for one: setup_inputs(seed, part) draws one part's arguments, and reference() takes and returns one part's arrays. A program takes and returns all parts, laid end to end along the dimension named above; each array names one. Nothing has to cross between parts.
All inputs are finite; a program needn't handle non-finite values.
Results may differ from the reference program's by a relative error of at most 0.0068.
Values may be sent and summed in bfloat16 or wider, within the bound.
A program may use at most 128 MiB of HBM per device.

```python
import math
import jax
import jax.numpy as jnp
from jax import lax

KI = 64
KO = 64
LAYERS = 2
N_DEV = 640
N_TRAIN = 10240
QUERIES = 128
N_EX = 16


def draw_train_features(key, part):
    key = jax.random.fold_in(key, 11)
    keys = jax.random.split(key, 6)
    shape = (LAYERS, N_TRAIN, KI, KO)
    noise = jnp.clip(jax.random.normal(keys[0], shape, jnp.float32), -4.0, 4.0)
    shared_out = jnp.clip(jax.random.normal(keys[1], (LAYERS, N_TRAIN, 1, KO), jnp.float32), -4.0, 4.0)
    shared_in = jnp.clip(jax.random.normal(keys[2], (LAYERS, N_TRAIN, KI, 1), jnp.float32), -4.0, 4.0)
    spread = math.log(10.0)
    in_scale = jnp.exp(jax.random.uniform(keys[3], (LAYERS, 1, KI, 1), jnp.float32, -0.69, 0.69))
    out_scale = jnp.exp(jax.random.uniform(keys[4], (LAYERS, 1, 1, KO), jnp.float32, -0.69, 0.69))
    position = jnp.arange(N_TRAIN, dtype=jnp.float32) / max(N_TRAIN - 1, 1)
    ramp = (1.0 + 2.0 * position)[None, :, None, None]
    weight = (0.3 + 1.2 * position)[None, :, None, None]
    row_scale = jnp.exp(jax.random.uniform(keys[5], (LAYERS, N_TRAIN, 1, 1), jnp.float32, 0.0, spread))
    value = 0.125 * ramp * row_scale * in_scale * out_scale * (noise + weight * (shared_out + shared_in))
    return value.reshape(LAYERS, N_TRAIN, KI * KO).astype(jnp.bfloat16)


def draw_test_features(key, part):
    key = jax.random.fold_in(key, 23)
    keys = jax.random.split(key, 2)
    shape = (LAYERS, QUERIES, KI * KO)
    noise = jnp.clip(jax.random.normal(keys[0], shape, jnp.float32), -4.0, 4.0)
    spread = math.log(10.0)
    row_scale = jnp.exp(jax.random.uniform(keys[1], (LAYERS, QUERIES, 1), jnp.float32, 0.0, spread))
    return (noise * row_scale).astype(jnp.bfloat16)


def setup_inputs(seed: int = 0, part: int = 0) -> dict:
    key_list = jax.random.split(jax.random.key(seed), 3)
    part_keys = jax.random.split(jax.random.fold_in(key_list[2], part), 3)
    return {
        "train_features": draw_train_features(jax.random.fold_in(jax.random.fold_in(key_list[2], part), 71), part),
        "test_features": draw_test_features(jax.random.fold_in(jax.random.fold_in(key_list[2], part), 71), part),
    }


def inverse_factor(stats):
    size = stats.shape[0]
    identity_matrix = jnp.eye(size, dtype=jnp.float32)
    damped = stats + 0.1 * jnp.trace(stats) / size * identity_matrix
    factor = jnp.linalg.cholesky(damped)
    factor_inverse = lax.linalg.triangular_solve(factor, identity_matrix, left_side=True, lower=True)
    return jnp.dot(factor_inverse.T, factor_inverse, precision=lax.Precision.HIGHEST)

def precondition(block, left_inverse, right_inverse):
    count = block.shape[0]
    values = block.astype(jnp.float32).reshape(count, left_inverse.shape[0], right_inverse.shape[0])
    left = jnp.einsum('ij,rjo->rio', left_inverse, values, precision=lax.Precision.HIGHEST)
    right = jnp.einsum('rio,op->rip', left, right_inverse, precision=lax.Precision.HIGHEST)
    return right.reshape(count, -1).astype(jnp.bfloat16)

def reference(train_features, test_features):

    def block_rows(index):
        return lax.dynamic_slice_in_dim(train_features, (index * N_DEV).astype(jnp.int32), N_DEV, 1)

    def add_stats(carry, index):
        block = block_rows(index).astype(jnp.float32).reshape(LAYERS, N_DEV, KI, KO)
        inner = jnp.einsum('lnio,lnjo->lij', block, block, precision=lax.Precision.HIGHEST)
        outer = jnp.einsum('lnio,lnip->lop', block, block, precision=lax.Precision.HIGHEST)
        return ((carry[0] + inner, carry[1] + outer), None)
    start_stats = (jnp.zeros((LAYERS, KI, KI), jnp.float32), jnp.zeros((LAYERS, KO, KO), jnp.float32))
    indices = jnp.arange(N_EX, dtype=jnp.int32)
    (stats_in, stats_out), unused = lax.scan(add_stats, start_stats, indices)
    stats_in = stats_in / N_TRAIN
    stats_out = stats_out / N_TRAIN
    preconditioned = []
    for layer in range(LAYERS):
        left_inverse = inverse_factor(stats_in[layer])
        right_inverse = inverse_factor(stats_out[layer])
        preconditioned.append(precondition(test_features[layer], left_inverse, right_inverse))

    def block_scores(index):
        block = block_rows(index)
        total = jnp.zeros((N_DEV, QUERIES), jnp.float32)
        for layer in range(LAYERS):
            total = total + jnp.dot(block[layer].astype(jnp.float32), preconditioned[layer].T.astype(jnp.float32), preferred_element_type=jnp.float32)
        return total
    raw_scores = lax.map(block_scores, indices).reshape(N_TRAIN, QUERIES)
    power = lax.optimization_barrier(jnp.sum(raw_scores * raw_scores, axis=0))
    return (raw_scores * lax.rsqrt(power / N_TRAIN + 1e-06)).astype(jnp.bfloat16)
```

```python
import functools

import jax
import jax.numpy as jnp
from jax import lax
from jax.experimental import pallas as pl
from jax.experimental.pallas import tpu as pltpu
from jax.sharding import PartitionSpec as P

K = 64
FEATURES = K * K
LANES = 128
TILES = 16
PARTS = 4
WIDE = 256


def dot(a, b, dims=((1,), (0,))):
    return lax.dot_general(a, b, (dims, ((), ())), preferred_element_type=jnp.float32)


def loop(count, step):
    def run(index, carry):
        step(index)
        return carry

    lax.fori_loop(0, count, run, 0)


def fold(acc):
    half = acc[:LANES, :LANES] + acc[LANES:, LANES:]
    top, low = half[:K], half[K:]
    return top + pltpu.roll(low, K, 1), pltpu.roll(top, K, 1) + low


def kernel(
    n, total_rows, train_hbm, test_ref, out_ref,
    x, xt, acc_in, acc_out, gathered, queries, right, both, scores,
    stats, reduce_buf, reduced, state, power_buf,
    load_sem, gsend, grecv, rsend, rrecv, asend, arecv, psend, precv,
):
    layers, rows, _ = x.shape
    me = lax.axis_index("ex")
    row_blocks = rows // LANES
    query_blocks = queries.shape[1]
    owners = min(n, TILES)
    tile = 2 * K // owners
    part = FEATURES // PARTS

    def load(layer, piece):
        columns = pl.ds(piece * part, part)
        return pltpu.make_async_copy(
            train_hbm.at[layer, :, columns], x.at[layer, :, columns], load_sem.at[layer, piece]
        )

    def remote(src, dst, send, recv, target):
        return pltpu.make_async_remote_copy(
            src_ref=src, dst_ref=dst, send_sem=send, recv_sem=recv,
            device_id={"ex": target}, device_id_type=pl.DeviceIdType.MESH,
        )

    for layer in range(layers):
        for piece in range(PARTS):
            load(layer, piece).start()

    barrier = pltpu.get_barrier_semaphore()

    def greet(offset):
        pl.semaphore_signal(
            barrier, inc=1, device_id={"ex": lax.rem(me + offset + 1, n)},
            device_id_type=pl.DeviceIdType.MESH,
        )

    loop(n - 1, greet)
    gathered[me] = jnp.concatenate(
        [test_ref[layer].astype(jnp.float32) for layer in range(layers)], axis=0
    ).astype(jnp.bfloat16)
    pl.semaphore_wait(barrier, n - 1)

    groups = n // 4
    mine_a, mine_r = me // 4, me % 4
    mine_b, mine_c = mine_r // 2, mine_r % 2
    across = mine_a * 4 + (1 - mine_b) * 2 + mine_c
    beside = mine_a * 4 + mine_b * 2 + (1 - mine_c)

    def pass_on(slot, target, index):
        return remote(gathered.at[slot], gathered.at[slot], gsend.at[index], grecv.at[slot], target)

    def first(offset):
        pass_on(me, lax.rem(mine_a + offset + 1, groups) * 4 + mine_r, offset).start()

    loop(groups - 1, first)

    def forward_across():
        pass_on(me, across, groups - 1).start()

        def step(offset):
            slot = lax.rem(mine_a + groups - offset - 1, groups) * 4 + mine_r
            pass_on(slot, across, groups + offset).wait_recv()
            pass_on(slot, across, groups + offset).start()

        loop(groups - 1, step)

    def forward_beside():
        def own(offset):
            slot = lax.rem(mine_a + groups - offset, groups) * 4 + mine_r
            pass_on(slot, beside, 2 * groups - 1 + offset).start()

        loop(groups, own)

        def other(offset):
            slot = lax.rem(mine_a + groups - offset, groups) * 4 + (1 - mine_b) * 2 + mine_c
            pass_on(slot, beside, 3 * groups - 1 + offset).wait_recv()
            pass_on(slot, beside, 3 * groups - 1 + offset).start()

        loop(groups, other)

    def outer_stats(layer):
        acc_out[...] = jnp.zeros_like(acc_out)
        for piece in range(PARTS):
            load(layer, piece).wait()

            def step(index, piece=piece):
                start = pl.multiple_of(piece * part + index * WIDE, WIDE)
                block = x[layer, :, pl.ds(start, WIDE)]
                turned = block.T
                acc_out[...] += dot(turned, block)
                for r in range(row_blocks):
                    xt[pl.ds(pl.multiple_of(r * FEATURES + start, WIDE), WIDE), :] = turned[
                        :, r * LANES : (r + 1) * LANES
                    ].astype(jnp.float32)

            loop(part // WIDE, step)

    def inner_stats(layer):
        acc_in[...] = jnp.zeros_like(acc_in)

        def step(index):
            block = jnp.concatenate(
                [
                    jnp.concatenate(
                        [
                            xt[pl.ds(r * FEATURES + index * 4 + u, K, stride=K), :].astype(jnp.bfloat16)
                            for r in range(row_blocks)
                        ],
                        axis=1,
                    )
                    for u in range(4)
                ],
                axis=0,
            )
            acc_in[...] += dot(block, block, ((1,), (1,)))

        loop(K // 4, step)

    lane = lax.broadcasted_iota(jnp.int32, (K, LANES), 1)
    sub = lax.broadcasted_iota(jnp.int32, (K, LANES), 0)
    low_half = lane < K

    for layer in range(layers):
        outer_stats(layer)
        if layer == 0:
            forward_across()
        else:
            forward_beside()
        inner_stats(layer)
        stats[layer * K : (layer + 1) * K, :] = jnp.where(
            low_half, fold(acc_in[...])[0], fold(acc_out[...])[1]
        )

    def tile_rows(owner):
        return pl.ds(pl.multiple_of(owner * tile, tile), tile)

    def to_owner(owner):
        return remote(stats.at[tile_rows(owner)], reduce_buf.at[me], rsend.at[owner], rrecv.at[me], owner)

    def only(condition, action):
        if owners == n:
            action()
        else:
            pl.when(condition)(action)

    def send_tile(offset):
        owner = lax.rem(me + offset + 1, n)
        only(owner < owners, lambda: to_owner(owner).start())

    loop(n - 1, send_tile)

    def from_owner(owner, target, index):
        return remote(reduced.at[tile_rows(owner)], reduced.at[tile_rows(owner)], asend.at[index], arecv.at[owner], target)

    def reduce_own():
        reduce_buf[me] = stats[tile_rows(me), :]

        def arrive(offset):
            source = lax.rem(me + n - offset - 1, n)
            remote(reduce_buf.at[source], reduce_buf.at[source], rsend.at[0], rrecv.at[source], source).wait_recv()

        loop(n - 1, arrive)
        total = reduce_buf[0]
        for source in range(1, n):
            total = total + reduce_buf[source]
        reduced[tile_rows(me), :] = total / total_rows

        def spread(offset):
            from_owner(me, lax.rem(me + offset + 1, n), offset).start()

        loop(n - 1, spread)

    only(me < owners, reduce_own)

    def arrive_beside(offset):
        slot = offset * 2 + (1 - mine_c)
        pass_on(slot, beside, 0).wait_recv()

    loop(n // 2, arrive_beside)

    per_block = LANES // 8

    def turn_queries(index):
        start = pl.multiple_of(index * LANES, LANES)
        for block in range(query_blocks):
            values = gathered[block * per_block : (block + 1) * per_block, :, pl.ds(start, LANES)].astype(jnp.float32)
            for layer in range(layers):
                turned = values[:, layer * 8 : (layer + 1) * 8, :].reshape(LANES, LANES).T
                queries[layer, block, pl.ds(start, LANES), :] = turned.astype(jnp.bfloat16)

    loop(FEATURES // LANES, turn_queries)

    def arrive_total(offset):
        owner = lax.rem(me + n - offset - 1, n)
        only(owner < owners, lambda: from_owner(owner, owner, 0).wait_recv())

    loop(n - 1, arrive_total)

    for layer in range(layers):
        value = reduced[layer * K : (layer + 1) * K, :]
        diagonal = (lane == sub) | (lane == sub + K)
        on = jnp.where(diagonal, value, 0.0)
        trace_in = jnp.sum(jnp.where(low_half, on, 0.0))
        trace_out = jnp.sum(jnp.where(low_half, 0.0, on))
        damping = 0.1 * jnp.where(low_half, trace_in, trace_out) / K
        state[layer] = jnp.where(diagonal, value + damping, value)

    def sweep(k):
        at_low, at_high, at_row = lane == k, lane == k + K, sub == k
        at_column = at_low | at_high
        for layer in range(layers):
            value = state[layer]
            row = state[layer, pl.ds(k, 1), :]
            column = jnp.where(
                low_half,
                jnp.sum(jnp.where(at_low, value, 0.0), axis=1, keepdims=True),
                jnp.sum(jnp.where(at_high, value, 0.0), axis=1, keepdims=True),
            )
            pivot = jnp.where(
                low_half[:1],
                jnp.sum(jnp.where(at_low[:1], row, 0.0), axis=1, keepdims=True),
                jnp.sum(jnp.where(at_high[:1], row, 0.0), axis=1, keepdims=True),
            )
            inverse = 1.0 / pivot
            scaled = row * inverse
            new = jnp.where(at_column, column * inverse, value - column * scaled)
            state[layer] = jnp.where(at_row, jnp.where(at_column, -inverse, scaled), new)

    loop(K, sweep)

    scores[...] = jnp.zeros_like(scores)
    for layer in range(layers):
        inverse = -state[layer]
        high = inverse.astype(jnp.bfloat16).astype(jnp.float32)
        rest = inverse - high
        right_pair = jnp.where(low_half, pltpu.roll(high, K, 1), rest).astype(jnp.bfloat16)
        left_pair = jnp.where(low_half, high, pltpu.roll(rest, K, 1)).astype(jnp.bfloat16)
        left_four = jnp.concatenate([left_pair, left_pair], axis=1)
        for block in range(query_blocks):

            def apply_right(index, layer=layer, block=block):
                start = pl.multiple_of(index * 4 * K, 4 * K)
                wide = [queries[layer, block, pl.ds(start + u * K, K), :] for u in range(4)]
                wide = jnp.concatenate(wide, axis=1)
                result = dot(right_pair, jnp.concatenate([wide, wide], axis=0))
                for u in range(4):
                    right[pl.ds(pl.multiple_of(start + u * K, K), K), :] = result[:, u * LANES : (u + 1) * LANES]

            loop(K // 4, apply_right)

            def apply_left(index):
                value = jnp.concatenate(
                    [right[pl.ds(index * 4 + u, K, stride=K), :] for u in range(4)], axis=1
                )
                upper = value.astype(jnp.bfloat16)
                lower = (value - upper.astype(jnp.float32)).astype(jnp.bfloat16)
                result = dot(left_four, jnp.concatenate([upper, upper, lower, lower], axis=0))
                for u in range(4):
                    both[pl.ds(index * 4 + u, K, stride=K), :] = result[:, u * LANES : (u + 1) * LANES]

            loop(K // 4, apply_left)

            def score(index, layer=layer, block=block):
                start = pl.multiple_of(index * 512, 512)
                scores[block] += dot(
                    x[layer, :, pl.ds(start, 512)], both[pl.ds(start, 512), :].astype(jnp.bfloat16)
                )

            loop(FEATURES // 512, score)

    for block in range(query_blocks):
        value = scores[block]
        power_buf[me, :, block * LANES : (block + 1) * LANES] = jnp.broadcast_to(
            jnp.sum(value * value, axis=0, keepdims=True), (8, LANES)
        )

    def send_power(offset):
        target = lax.rem(me + offset + 1, n)
        remote(power_buf.at[me], power_buf.at[me], psend.at[offset], precv.at[me], target).start()

    loop(n - 1, send_power)

    def arrive_power(offset):
        source = lax.rem(me + n - offset - 1, n)
        remote(power_buf.at[source], power_buf.at[source], psend.at[0], precv.at[source], source).wait_recv()

    loop(n - 1, arrive_power)
    power = power_buf[0]
    for source in range(1, n):
        power = power + power_buf[source]
    scale = lax.rsqrt(power / total_rows + 1e-06)
    for block in range(query_blocks):
        columns = slice(block * LANES, (block + 1) * LANES)
        out_ref[:, columns] = (scores[block] * scale[:1, columns]).astype(out_ref.dtype)

    def sent_queries(index):
        pass_on(me, beside, index).wait_send()

    loop(n - 1, sent_queries)

    def sent_tile(offset):
        owner = lax.rem(me + offset + 1, n)
        only(owner < owners, lambda: to_owner(owner).wait_send())

    loop(n - 1, sent_tile)

    def sent_total():
        loop(n - 1, lambda offset: from_owner(me, beside, offset).wait_send())

    only(me < owners, sent_total)

    def sent_power(offset):
        remote(power_buf.at[me], power_buf.at[me], psend.at[offset], precv.at[me], beside).wait_send()

    loop(n - 1, sent_power)


def body(train_features, test_features):
    layers, rows, features = train_features.shape
    count = test_features.shape[1]
    n = lax.axis_size("ex")
    query_count = count * n
    query_blocks = query_count // LANES
    owners = min(n, TILES)
    f32, bf16 = jnp.float32, jnp.bfloat16
    dma = pltpu.SemaphoreType.DMA
    return pl.pallas_call(
        functools.partial(kernel, n, rows * n),
        out_shape=jax.ShapeDtypeStruct((rows, query_count), bf16),
        in_specs=[pl.BlockSpec(memory_space=pl.ANY), pl.BlockSpec(memory_space=pltpu.VMEM)],
        out_specs=pl.BlockSpec(memory_space=pltpu.VMEM),
        scratch_shapes=[
            pltpu.VMEM((layers, rows, features), bf16),
            pltpu.VMEM((rows // LANES * features, LANES), f32),
            pltpu.VMEM((WIDE, WIDE), f32),
            pltpu.VMEM((WIDE, WIDE), f32),
            pltpu.VMEM((n, layers * count, features), bf16),
            pltpu.VMEM((layers, query_blocks, features, LANES), bf16),
            pltpu.VMEM((features, LANES), f32),
            pltpu.VMEM((features, LANES), f32),
            pltpu.VMEM((query_blocks, rows, LANES), f32),
            pltpu.VMEM((layers * K, LANES), f32),
            pltpu.VMEM((n, layers * K // owners, LANES), f32),
            pltpu.VMEM((layers * K, LANES), f32),
            pltpu.VMEM((layers, K, LANES), f32),
            pltpu.VMEM((n, 8, query_count), f32),
            dma((layers, PARTS)),
            dma((n,)), dma((n,)), dma((n,)), dma((n,)),
            dma((n,)), dma((n,)), dma((n,)), dma((n,)),
        ],
        compiler_params=pltpu.CompilerParams(
            collective_id=0, has_side_effects=True, vmem_limit_bytes=60 * 1024 * 1024
        ),
    )(train_features, test_features)


def solution(mesh):
    in_specs = (P(None, ("grp", "ex"), None), P(None, ("grp", "ex"), None))
    out_specs = P(("grp", "ex"), None)
    return jax.shard_map(body, mesh=mesh, in_specs=in_specs, out_specs=out_specs, check_vma=False)
```

```python
import functools

import jax
import jax.numpy as jnp
from jax import lax
from jax.experimental import pallas as pl
from jax.experimental.pallas import tpu as pltpu
from jax.sharding import PartitionSpec as P

K = 64
FEATURES = K * K
LANES = 128
TILES = 16
PARTS = 4
WIDE = 256
PITCH = K + 1


def dot(a, b, dims=((1,), (0,))):
    return lax.dot_general(a, b, (dims, ((), ())), preferred_element_type=jnp.float32)


def loop(count, step):
    def run(index, carry):
        step(index)
        return carry

    lax.fori_loop(0, count, run, 0)


def fold(acc):
    half = acc[:LANES, :LANES] + acc[LANES:, LANES:]
    top, low = half[:K], half[K:]
    return top + pltpu.roll(low, K, 1), pltpu.roll(top, K, 1) + low


def kernel(
    n, total_rows, train_hbm, test_ref, out_ref,
    x, xt, acc_in, acc_out, gathered, queries, right, both, scores,
    stats, reduce_buf, reduced, state, power_buf,
    load_sem, gsend, grecv, rsend, rrecv, asend, arecv, psend, precv,
):
    layers, rows, _ = x.shape
    me = lax.axis_index("ex")
    row_blocks = rows // LANES
    query_blocks = queries.shape[1]
    owners = min(n, TILES)
    tile = 2 * K // owners
    part = FEATURES // PARTS

    def load(layer, piece):
        columns = pl.ds(piece * part, part)
        return pltpu.make_async_copy(
            train_hbm.at[layer, :, columns], x.at[layer, :, columns], load_sem.at[layer, piece]
        )

    def remote(src, dst, send, recv, target):
        return pltpu.make_async_remote_copy(
            src_ref=src, dst_ref=dst, send_sem=send, recv_sem=recv,
            device_id={"ex": target}, device_id_type=pl.DeviceIdType.MESH,
        )

    for layer in range(layers):
        for piece in range(PARTS):
            load(layer, piece).start()

    barrier = pltpu.get_barrier_semaphore()

    def greet(offset):
        pl.semaphore_signal(
            barrier, inc=1, device_id={"ex": lax.rem(me + offset + 1, n)},
            device_id_type=pl.DeviceIdType.MESH,
        )

    loop(n - 1, greet)
    gathered[me] = jnp.concatenate(
        [test_ref[layer].astype(jnp.float32) for layer in range(layers)], axis=0
    ).astype(jnp.bfloat16)
    pl.semaphore_wait(barrier, n - 1)

    groups = n // 4
    mine_a, mine_r = me // 4, me % 4
    mine_b, mine_c = mine_r // 2, mine_r % 2
    across = mine_a * 4 + (1 - mine_b) * 2 + mine_c
    beside = mine_a * 4 + mine_b * 2 + (1 - mine_c)

    def pass_on(slot, target, index):
        return remote(gathered.at[slot], gathered.at[slot], gsend.at[index], grecv.at[slot], target)

    def first(offset):
        pass_on(me, lax.rem(mine_a + offset + 1, groups) * 4 + mine_r, offset).start()

    loop(groups - 1, first)
    pass_on(me, across, groups - 1).start()
    pass_on(me, beside, 2 * groups - 1).start()

    def forward_across():
        def step(offset):
            slot = lax.rem(mine_a + groups - offset - 1, groups) * 4 + mine_r
            pass_on(slot, across, groups + offset).wait_recv()
            pass_on(slot, across, groups + offset).start()

        loop(groups - 1, step)

    def forward_beside():
        def own(offset):
            slot = lax.rem(mine_a + groups - offset - 1, groups) * 4 + mine_r
            pass_on(slot, beside, 2 * groups + offset).start()

        loop(groups - 1, own)

        def other(offset):
            slot = lax.rem(mine_a + groups - offset, groups) * 4 + (1 - mine_b) * 2 + mine_c
            pass_on(slot, beside, 3 * groups - 1 + offset).wait_recv()
            pass_on(slot, beside, 3 * groups - 1 + offset).start()

        loop(groups, other)

    def outer_stats(layer):
        acc_out[...] = jnp.zeros_like(acc_out)
        for piece in range(PARTS):
            load(layer, piece).wait()

            def step(index, piece=piece):
                start = pl.multiple_of(piece * part + index * WIDE, WIDE)
                block = x[layer, :, pl.ds(start, WIDE)]
                turned = block.T
                acc_out[...] += dot(turned, block)
                first_block = piece * (part // K) + index * (WIDE // K)
                for r in range(row_blocks):
                    for u in range(WIDE // K):
                        xt[pl.ds((r * K + first_block + u) * PITCH, K), :] = turned[
                            u * K : (u + 1) * K, r * LANES : (r + 1) * LANES
                        ].astype(jnp.float32)

            loop(part // WIDE, step)

    def inner_stats(layer):
        acc_in[...] = jnp.zeros_like(acc_in)

        def step(index):
            block = jnp.concatenate(
                [
                    jnp.concatenate(
                        [
                            xt[pl.ds(r * K * PITCH + index * 4 + u, K, stride=PITCH), :].astype(jnp.bfloat16)
                            for r in range(row_blocks)
                        ],
                        axis=1,
                    )
                    for u in range(4)
                ],
                axis=0,
            )
            acc_in[...] += dot(block, block, ((1,), (1,)))

        loop(K // 4, step)

    lane = lax.broadcasted_iota(jnp.int32, (K, LANES), 1)
    sub = lax.broadcasted_iota(jnp.int32, (K, LANES), 0)
    low_half = lane < K

    for layer in range(layers):
        outer_stats(layer)
        inner_stats(layer)
        if layer == 0:
            forward_across()
        stats[layer * K : (layer + 1) * K, :] = jnp.where(
            low_half, fold(acc_in[...])[0], fold(acc_out[...])[1]
        )

    def tile_rows(owner):
        return pl.ds(pl.multiple_of(owner * tile, tile), tile)

    def to_owner(owner):
        return remote(stats.at[tile_rows(owner)], reduce_buf.at[me], rsend.at[owner], rrecv.at[me], owner)

    def only(condition, action):
        if owners == n:
            action()
        else:
            pl.when(condition)(action)

    def send_tile(offset):
        owner = lax.rem(me + offset + 1, n)
        only(owner < owners, lambda: to_owner(owner).start())

    loop(n - 1, send_tile)
    forward_beside()

    def from_owner(owner, target, index):
        return remote(reduced.at[tile_rows(owner)], reduced.at[tile_rows(owner)], asend.at[index], arecv.at[owner], target)

    def reduce_own():
        reduce_buf[me] = stats[tile_rows(me), :]

        def arrive(offset):
            source = lax.rem(me + n - offset - 1, n)
            remote(reduce_buf.at[source], reduce_buf.at[source], rsend.at[0], rrecv.at[source], source).wait_recv()

        loop(n - 1, arrive)
        total = reduce_buf[0]
        for source in range(1, n):
            total = total + reduce_buf[source]
        reduced[tile_rows(me), :] = total / total_rows

        def spread(offset):
            from_owner(me, lax.rem(me + offset + 1, n), offset).start()

        loop(n - 1, spread)

    only(me < owners, reduce_own)

    def arrive_beside(offset):
        slot = offset * 2 + (1 - mine_c)
        pass_on(slot, beside, 0).wait_recv()

    loop(n // 2, arrive_beside)

    per_block = LANES // 8

    def turn_queries(index):
        start = pl.multiple_of(index * LANES, LANES)
        for block in range(query_blocks):
            values = gathered[block * per_block : (block + 1) * per_block, :, pl.ds(start, LANES)].astype(jnp.float32)
            for layer in range(layers):
                turned = values[:, layer * 8 : (layer + 1) * 8, :].reshape(LANES, LANES).T
                queries[layer, block, pl.ds(start, LANES), :] = turned.astype(jnp.bfloat16)

    loop(FEATURES // LANES, turn_queries)

    def arrive_total(offset):
        owner = lax.rem(me + n - offset - 1, n)
        only(owner < owners, lambda: from_owner(owner, owner, 0).wait_recv())

    loop(n - 1, arrive_total)

    for layer in range(layers):
        value = reduced[layer * K : (layer + 1) * K, :]
        diagonal = (lane == sub) | (lane == sub + K)
        on = jnp.where(diagonal, value, 0.0)
        trace_in = jnp.sum(jnp.where(low_half, on, 0.0))
        trace_out = jnp.sum(jnp.where(low_half, 0.0, on))
        damping = 0.1 * jnp.where(low_half, trace_in, trace_out) / K
        state[layer] = jnp.where(diagonal, value + damping, value)

    def sweep(k):
        place = jnp.where(low_half, k, k + K)
        at_column, at_row = lane == place, sub == k
        for layer in range(layers):
            value = state[layer]
            row = state[layer, pl.ds(k, 1), :]
            column = jnp.take_along_axis(value, place, axis=1, mode="promise_in_bounds")
            pivot = jnp.take_along_axis(
                jnp.broadcast_to(row, (8, LANES)), place[:8], axis=1, mode="promise_in_bounds"
            )
            inverse = 1.0 / pivot[:1]
            scaled = row * inverse
            new = jnp.where(at_column, column * inverse, value - column * scaled)
            state[layer] = jnp.where(at_row, jnp.where(at_column, -inverse, scaled), new)

    loop(K, sweep)

    scores[...] = jnp.zeros_like(scores)
    for layer in range(layers):
        inverse = -state[layer]
        high = inverse.astype(jnp.bfloat16).astype(jnp.float32)
        rest = inverse - high
        right_pair = jnp.where(low_half, pltpu.roll(high, K, 1), rest).astype(jnp.bfloat16)
        left_pair = jnp.where(low_half, high, pltpu.roll(rest, K, 1)).astype(jnp.bfloat16)
        left_four = jnp.concatenate([left_pair, left_pair], axis=1)
        for block in range(query_blocks):

            def apply_right(index, layer=layer, block=block):
                start = pl.multiple_of(index * 4 * K, 4 * K)
                wide = [queries[layer, block, pl.ds(start + u * K, K), :] for u in range(4)]
                wide = jnp.concatenate(wide, axis=1)
                result = dot(right_pair, jnp.concatenate([wide, wide], axis=0))
                for u in range(4):
                    right[pl.ds((index * 4 + u) * PITCH, K), :] = result[:, u * LANES : (u + 1) * LANES]

            loop(K // 4, apply_right)

            def apply_left(index):
                value = jnp.concatenate(
                    [right[pl.ds(index * 4 + u, K, stride=PITCH), :] for u in range(4)], axis=1
                )
                upper = value.astype(jnp.bfloat16)
                lower = (value - upper.astype(jnp.float32)).astype(jnp.bfloat16)
                result = dot(left_four, jnp.concatenate([upper, upper, lower, lower], axis=0))
                for u in range(4):
                    both[pl.ds(index * 4 + u, K, stride=PITCH), :] = result[:, u * LANES : (u + 1) * LANES]

            loop(K // 4, apply_left)

            def score(index, layer=layer, block=block):
                start = pl.multiple_of(index * 512, 512)
                weights = [
                    both[pl.ds((index * 8 + u) * PITCH, K), :].astype(jnp.bfloat16) for u in range(8)
                ]
                scores[block] += dot(x[layer, :, pl.ds(start, 512)], jnp.concatenate(weights, axis=0))

            loop(FEATURES // 512, score)

    for block in range(query_blocks):
        value = scores[block]
        power_buf[me, :, block * LANES : (block + 1) * LANES] = jnp.broadcast_to(
            jnp.sum(value * value, axis=0, keepdims=True), (8, LANES)
        )

    def send_power(offset):
        target = lax.rem(me + offset + 1, n)
        remote(power_buf.at[me], power_buf.at[me], psend.at[offset], precv.at[me], target).start()

    loop(n - 1, send_power)

    def arrive_power(offset):
        source = lax.rem(me + n - offset - 1, n)
        remote(power_buf.at[source], power_buf.at[source], psend.at[0], precv.at[source], source).wait_recv()

    loop(n - 1, arrive_power)
    power = power_buf[0]
    for source in range(1, n):
        power = power + power_buf[source]
    scale = lax.rsqrt(power / total_rows + 1e-06)
    for block in range(query_blocks):
        columns = slice(block * LANES, (block + 1) * LANES)
        out_ref[:, columns] = (scores[block] * scale[:1, columns]).astype(out_ref.dtype)

    def sent_queries(index):
        pass_on(me, beside, index).wait_send()

    loop(n - 1, sent_queries)

    def sent_tile(offset):
        owner = lax.rem(me + offset + 1, n)
        only(owner < owners, lambda: to_owner(owner).wait_send())

    loop(n - 1, sent_tile)

    def sent_total():
        loop(n - 1, lambda offset: from_owner(me, beside, offset).wait_send())

    only(me < owners, sent_total)

    def sent_power(offset):
        remote(power_buf.at[me], power_buf.at[me], psend.at[offset], precv.at[me], beside).wait_send()

    loop(n - 1, sent_power)


def body(train_features, test_features):
    layers, rows, features = train_features.shape
    count = test_features.shape[1]
    n = lax.axis_size("ex")
    query_count = count * n
    query_blocks = query_count // LANES
    owners = min(n, TILES)
    f32, bf16 = jnp.float32, jnp.bfloat16
    dma = pltpu.SemaphoreType.DMA
    return pl.pallas_call(
        functools.partial(kernel, n, rows * n),
        out_shape=jax.ShapeDtypeStruct((rows, query_count), bf16),
        in_specs=[pl.BlockSpec(memory_space=pl.ANY), pl.BlockSpec(memory_space=pltpu.VMEM)],
        out_specs=pl.BlockSpec(memory_space=pltpu.VMEM),
        scratch_shapes=[
            pltpu.VMEM((layers, rows, features), bf16),
            pltpu.VMEM((rows // LANES * K * PITCH, LANES), f32),
            pltpu.VMEM((WIDE, WIDE), f32),
            pltpu.VMEM((WIDE, WIDE), f32),
            pltpu.VMEM((n, layers * count, features), bf16),
            pltpu.VMEM((layers, query_blocks, features, LANES), bf16),
            pltpu.VMEM((K * PITCH, LANES), f32),
            pltpu.VMEM((K * PITCH, LANES), f32),
            pltpu.VMEM((query_blocks, rows, LANES), f32),
            pltpu.VMEM((layers * K, LANES), f32),
            pltpu.VMEM((n, layers * K // owners, LANES), f32),
            pltpu.VMEM((layers * K, LANES), f32),
            pltpu.VMEM((layers, K, LANES), f32),
            pltpu.VMEM((n, 8, query_count), f32),
            dma((layers, PARTS)),
            dma((n,)), dma((n,)), dma((n,)), dma((n,)),
            dma((n,)), dma((n,)), dma((n,)), dma((n,)),
        ],
        compiler_params=pltpu.CompilerParams(
            collective_id=0, has_side_effects=True, vmem_limit_bytes=60 * 1024 * 1024
        ),
    )(train_features, test_features)


def solution(mesh):
    in_specs = (P(None, ("grp", "ex"), None), P(None, ("grp", "ex"), None))
    out_specs = P(("grp", "ex"), None)
    return jax.shard_map(body, mesh=mesh, in_specs=in_specs, out_specs=out_specs, check_vma=False)
```

```python
import functools

import jax
import jax.numpy as jnp
from jax import lax
from jax.experimental import pallas as pl
from jax.experimental.pallas import tpu as pltpu
from jax.sharding import PartitionSpec as P

K = 64
FEATURES = K * K
LANES = 128
TILES = 16
PARTS = 4
WIDE = 256
PITCH = K + 1


def dot(a, b, dims=((1,), (0,))):
    return lax.dot_general(a, b, (dims, ((), ())), preferred_element_type=jnp.float32)


def loop(count, step, together=1):
    def run(index, carry):
        for u in range(together):
            step(index * together + u)
        return carry

    lax.fori_loop(0, count // together, run, 0)


def fold(acc):
    half = acc[:LANES, :LANES] + acc[LANES:, LANES:]
    top, low = half[:K], half[K:]
    return top + pltpu.roll(low, K, 1), pltpu.roll(top, K, 1) + low


def kernel(
    n, total_rows, train_hbm, test_ref, out_ref,
    x, xt, acc_in, acc_out, gathered, queries, right, both, scores,
    stats, reduce_buf, reduced, power_buf,
    load_sem, gsend, grecv, rsend, rrecv, asend, arecv, psend, precv,
):
    layers, rows, _ = x.shape
    me = lax.axis_index("ex")
    row_blocks = rows // LANES
    query_blocks = queries.shape[1]
    owners = min(n, TILES)
    tile = 2 * K // owners
    part = FEATURES // PARTS

    def load(layer, piece):
        columns = pl.ds(piece * part, part)
        return pltpu.make_async_copy(
            train_hbm.at[layer, :, columns], x.at[layer, :, columns], load_sem.at[layer, piece]
        )

    def remote(src, dst, send, recv, target):
        return pltpu.make_async_remote_copy(
            src_ref=src, dst_ref=dst, send_sem=send, recv_sem=recv,
            device_id={"ex": target}, device_id_type=pl.DeviceIdType.MESH,
        )

    for layer in range(layers):
        for piece in range(PARTS):
            load(layer, piece).start()

    barrier = pltpu.get_barrier_semaphore()

    def greet(offset):
        pl.semaphore_signal(
            barrier, inc=1, device_id={"ex": lax.rem(me + offset + 1, n)},
            device_id_type=pl.DeviceIdType.MESH,
        )

    loop(n - 1, greet)
    gathered[me] = jnp.concatenate(
        [test_ref[layer].astype(jnp.float32) for layer in range(layers)], axis=0
    ).astype(jnp.bfloat16)
    pl.semaphore_wait(barrier, n - 1)

    groups = n // 4
    mine_a, mine_r = me // 4, me % 4
    mine_b, mine_c = mine_r // 2, mine_r % 2
    across = mine_a * 4 + (1 - mine_b) * 2 + mine_c
    beside = mine_a * 4 + mine_b * 2 + (1 - mine_c)

    def pass_on(slot, target, index):
        return remote(gathered.at[slot], gathered.at[slot], gsend.at[index], grecv.at[slot], target)

    def first(offset):
        pass_on(me, lax.rem(mine_a + offset + 1, groups) * 4 + mine_r, offset).start()

    loop(groups - 1, first)
    pass_on(me, across, groups - 1).start()
    pass_on(me, beside, 2 * groups - 1).start()

    def forward_across():
        def step(offset):
            slot = lax.rem(mine_a + groups - offset - 1, groups) * 4 + mine_r
            pass_on(slot, across, groups + offset).wait_recv()
            pass_on(slot, across, groups + offset).start()

        loop(groups - 1, step)

    def forward_beside():
        def own(offset):
            slot = lax.rem(mine_a + groups - offset - 1, groups) * 4 + mine_r
            pass_on(slot, beside, 2 * groups + offset).start()

        loop(groups - 1, own)

        def other(offset):
            slot = lax.rem(mine_a + groups - offset, groups) * 4 + (1 - mine_b) * 2 + mine_c
            pass_on(slot, beside, 3 * groups - 1 + offset).wait_recv()
            pass_on(slot, beside, 3 * groups - 1 + offset).start()

        loop(groups, other)

    def outer_stats(layer):
        acc_out[...] = jnp.zeros_like(acc_out)
        for piece in range(PARTS):
            load(layer, piece).wait()

            def step(index, piece=piece):
                start = pl.multiple_of(piece * part + index * WIDE, WIDE)
                block = x[layer, :, pl.ds(start, WIDE)]
                turned = block.T
                acc_out[...] += dot(turned, block)
                first_block = piece * (part // K) + index * (WIDE // K)
                for r in range(row_blocks):
                    for u in range(WIDE // K):
                        xt[pl.ds((r * K + first_block + u) * PITCH, K), :] = turned[
                            u * K : (u + 1) * K, r * LANES : (r + 1) * LANES
                        ].astype(jnp.float32)

            loop(part // WIDE, step, 2)

    def inner_stats(layer):
        acc_in[...] = jnp.zeros_like(acc_in)

        def step(index):
            block = jnp.concatenate(
                [
                    jnp.concatenate(
                        [
                            xt[pl.ds(r * K * PITCH + index * 4 + u, K, stride=PITCH), :].astype(jnp.bfloat16)
                            for r in range(row_blocks)
                        ],
                        axis=1,
                    )
                    for u in range(4)
                ],
                axis=0,
            )
            acc_in[...] += dot(block, block, ((1,), (1,)))

        loop(K // 4, step, 2)

    lane = lax.broadcasted_iota(jnp.int32, (K, LANES), 1)
    sub = lax.broadcasted_iota(jnp.int32, (K, LANES), 0)
    low_half = lane < K

    for layer in range(layers):
        outer_stats(layer)
        inner_stats(layer)
        if layer == 0:
            forward_across()
        stats[layer * K : (layer + 1) * K, :] = jnp.where(
            low_half, fold(acc_in[...])[0], fold(acc_out[...])[1]
        )

    def tile_rows(owner):
        return pl.ds(pl.multiple_of(owner * tile, tile), tile)

    def to_owner(owner):
        return remote(stats.at[tile_rows(owner)], reduce_buf.at[me], rsend.at[owner], rrecv.at[me], owner)

    def only(condition, action):
        if owners == n:
            action()
        else:
            pl.when(condition)(action)

    def send_tile(offset):
        owner = lax.rem(me + offset + 1, n)
        only(owner < owners, lambda: to_owner(owner).start())

    loop(n - 1, send_tile)
    forward_beside()

    def from_owner(owner, target, index):
        return remote(reduced.at[tile_rows(owner)], reduced.at[tile_rows(owner)], asend.at[index], arecv.at[owner], target)

    def reduce_own():
        reduce_buf[me] = stats[tile_rows(me), :]

        def arrive(offset):
            source = lax.rem(me + n - offset - 1, n)
            remote(reduce_buf.at[source], reduce_buf.at[source], rsend.at[0], rrecv.at[source], source).wait_recv()

        loop(n - 1, arrive)
        total = reduce_buf[0]
        for source in range(1, n):
            total = total + reduce_buf[source]
        reduced[tile_rows(me), :] = total / total_rows

        def spread(offset):
            from_owner(me, lax.rem(me + offset + 1, n), offset).start()

        loop(n - 1, spread)

    only(me < owners, reduce_own)

    def arrive_beside(offset):
        slot = offset * 2 + (1 - mine_c)
        pass_on(slot, beside, 0).wait_recv()

    loop(n // 2, arrive_beside)

    per_block = LANES // 8

    def turn_queries(index):
        start = pl.multiple_of(index * LANES, LANES)
        for block in range(query_blocks):
            values = gathered[block * per_block : (block + 1) * per_block, :, pl.ds(start, LANES)].astype(jnp.float32)
            for layer in range(layers):
                turned = values[:, layer * 8 : (layer + 1) * 8, :].reshape(LANES, LANES).T
                queries[layer, block, pl.ds(start, LANES), :] = turned.astype(jnp.bfloat16)

    loop(FEATURES // LANES, turn_queries)

    def arrive_total(offset):
        owner = lax.rem(me + n - offset - 1, n)
        only(owner < owners, lambda: from_owner(owner, owner, 0).wait_recv())

    loop(n - 1, arrive_total)

    states = []
    for layer in range(layers):
        value = reduced[layer * K : (layer + 1) * K, :]
        diagonal = (lane == sub) | (lane == sub + K)
        on = jnp.where(diagonal, value, 0.0)
        trace_in = jnp.sum(jnp.where(low_half, on, 0.0))
        trace_out = jnp.sum(jnp.where(low_half, 0.0, on))
        damping = 0.1 * jnp.where(low_half, trace_in, trace_out) / K
        states.append(jnp.where(diagonal, value + damping, value))

    for k in range(K):
        place = jnp.where(low_half, k, k + K)
        at_column, at_row = lane == place, sub == k
        for layer in range(layers):
            value = states[layer]
            row = value[k : k + 1]
            column = jnp.take_along_axis(value, place, axis=1, mode="promise_in_bounds")
            pivot = jnp.take_along_axis(
                jnp.broadcast_to(row, (8, LANES)), place[:8], axis=1, mode="promise_in_bounds"
            )
            inverse = 1.0 / pivot[:1]
            scaled = row * inverse
            new = jnp.where(at_column, column * inverse, value - column * scaled)
            states[layer] = jnp.where(at_row, jnp.where(at_column, -inverse, scaled), new)

    scores[...] = jnp.zeros_like(scores)
    for layer in range(layers):
        inverse = -states[layer]
        high = inverse.astype(jnp.bfloat16).astype(jnp.float32)
        rest = inverse - high
        right_pair = jnp.where(low_half, pltpu.roll(high, K, 1), rest).astype(jnp.bfloat16)
        left_pair = jnp.where(low_half, high, pltpu.roll(rest, K, 1)).astype(jnp.bfloat16)
        left_four = jnp.concatenate([left_pair, left_pair], axis=1)
        for block in range(query_blocks):

            def apply_right(index, layer=layer, block=block):
                start = pl.multiple_of(index * 4 * K, 4 * K)
                wide = [queries[layer, block, pl.ds(start + u * K, K), :] for u in range(4)]
                wide = jnp.concatenate(wide, axis=1)
                result = dot(right_pair, jnp.concatenate([wide, wide], axis=0))
                for u in range(4):
                    right[pl.ds((index * 4 + u) * PITCH, K), :] = result[:, u * LANES : (u + 1) * LANES]

            loop(K // 4, apply_right, 4)

            def apply_left(index):
                value = jnp.concatenate(
                    [right[pl.ds(index * 4 + u, K, stride=PITCH), :] for u in range(4)], axis=1
                )
                upper = value.astype(jnp.bfloat16)
                lower = (value - upper.astype(jnp.float32)).astype(jnp.bfloat16)
                result = dot(left_four, jnp.concatenate([upper, upper, lower, lower], axis=0))
                for u in range(4):
                    both[pl.ds(index * 4 + u, K, stride=PITCH), :] = result[:, u * LANES : (u + 1) * LANES]

            loop(K // 4, apply_left, 4)

            def score(index, layer=layer, block=block):
                start = pl.multiple_of(index * 1024, 1024)
                weights = [
                    both[pl.ds((index * 16 + u) * PITCH, K), :].astype(jnp.bfloat16) for u in range(16)
                ]
                scores[block] += dot(x[layer, :, pl.ds(start, 1024)], jnp.concatenate(weights, axis=0))

            loop(FEATURES // 1024, score)

    for block in range(query_blocks):
        value = scores[block]
        power_buf[me, :, block * LANES : (block + 1) * LANES] = jnp.broadcast_to(
            jnp.sum(value * value, axis=0, keepdims=True), (8, LANES)
        )

    def send_power(offset):
        target = lax.rem(me + offset + 1, n)
        remote(power_buf.at[me], power_buf.at[me], psend.at[offset], precv.at[me], target).start()

    loop(n - 1, send_power)

    def arrive_power(offset):
        source = lax.rem(me + n - offset - 1, n)
        remote(power_buf.at[source], power_buf.at[source], psend.at[0], precv.at[source], source).wait_recv()

    loop(n - 1, arrive_power)
    power = power_buf[0]
    for source in range(1, n):
        power = power + power_buf[source]
    scale = lax.rsqrt(power / total_rows + 1e-06)
    for block in range(query_blocks):
        columns = slice(block * LANES, (block + 1) * LANES)
        out_ref[:, columns] = (scores[block] * scale[:1, columns]).astype(out_ref.dtype)

    def sent_queries(index):
        pass_on(me, beside, index).wait_send()

    loop(n - 1, sent_queries)

    def sent_tile(offset):
        owner = lax.rem(me + offset + 1, n)
        only(owner < owners, lambda: to_owner(owner).wait_send())

    loop(n - 1, sent_tile)

    def sent_total():
        loop(n - 1, lambda offset: from_owner(me, beside, offset).wait_send())

    only(me < owners, sent_total)

    def sent_power(offset):
        remote(power_buf.at[me], power_buf.at[me], psend.at[offset], precv.at[me], beside).wait_send()

    loop(n - 1, sent_power)


def body(train_features, test_features):
    layers, rows, features = train_features.shape
    count = test_features.shape[1]
    n = lax.axis_size("ex")
    query_count = count * n
    query_blocks = query_count // LANES
    owners = min(n, TILES)
    f32, bf16 = jnp.float32, jnp.bfloat16
    dma = pltpu.SemaphoreType.DMA
    return pl.pallas_call(
        functools.partial(kernel, n, rows * n),
        out_shape=jax.ShapeDtypeStruct((rows, query_count), bf16),
        in_specs=[pl.BlockSpec(memory_space=pl.ANY), pl.BlockSpec(memory_space=pltpu.VMEM)],
        out_specs=pl.BlockSpec(memory_space=pltpu.VMEM),
        scratch_shapes=[
            pltpu.VMEM((layers, rows, features), bf16),
            pltpu.VMEM((rows // LANES * K * PITCH, LANES), f32),
            pltpu.VMEM((WIDE, WIDE), f32),
            pltpu.VMEM((WIDE, WIDE), f32),
            pltpu.VMEM((n, layers * count, features), bf16),
            pltpu.VMEM((layers, query_blocks, features, LANES), bf16),
            pltpu.VMEM((K * PITCH, LANES), f32),
            pltpu.VMEM((K * PITCH, LANES), f32),
            pltpu.VMEM((query_blocks, rows, LANES), f32),
            pltpu.VMEM((layers * K, LANES), f32),
            pltpu.VMEM((n, layers * K // owners, LANES), f32),
            pltpu.VMEM((layers * K, LANES), f32),
            pltpu.VMEM((n, 8, query_count), f32),
            dma((layers, PARTS)),
            dma((n,)), dma((n,)), dma((n,)), dma((n,)),
            dma((n,)), dma((n,)), dma((n,)), dma((n,)),
        ],
        compiler_params=pltpu.CompilerParams(
            collective_id=0, has_side_effects=True, vmem_limit_bytes=60 * 1024 * 1024
        ),
    )(train_features, test_features)


def solution(mesh):
    in_specs = (P(None, ("grp", "ex"), None), P(None, ("grp", "ex"), None))
    out_specs = P(("grp", "ex"), None)
    return jax.shard_map(body, mesh=mesh, in_specs=in_specs, out_specs=out_specs, check_vma=False)
```

```python
import functools

import jax
import jax.numpy as jnp
from jax import lax
from jax.experimental import pallas as pl
from jax.experimental.pallas import tpu as pltpu
from jax.sharding import PartitionSpec as P

K = 64
FEATURES = K * K
LANES = 128
TILES = 16
PARTS = 4
WIDE = 256
PITCH = K + 1


def dot(a, b, dims=((1,), (0,))):
    return lax.dot_general(a, b, (dims, ((), ())), preferred_element_type=jnp.float32)


def loop(count, step, together=1):
    def run(index, carry):
        for u in range(together):
            step(index * together + u)
        return carry

    lax.fori_loop(0, count // together, run, 0)


def fold(acc):
    half = acc[:LANES, :LANES] + acc[LANES:, LANES:]
    top, low = half[:K], half[K:]
    return top + pltpu.roll(low, K, 1), pltpu.roll(top, K, 1) + low


def kernel(
    n, total_rows, train_hbm, test_ref, out_ref,
    x, xt, acc_in, acc_out, gathered, queries, right, both, scores,
    stats, reduce_buf, reduced, power_buf,
    load_sem, gsend, grecv, rsend, rrecv, asend, arecv, psend, precv,
):
    layers, rows, _ = x.shape
    me = lax.axis_index("ex")
    row_blocks = rows // LANES
    query_blocks = queries.shape[1]
    owners = min(n, TILES)
    spread_out = 3 if n % 3 == 1 else 1
    tile = 2 * K // owners
    part = FEATURES // PARTS

    def load(layer, piece):
        columns = pl.ds(piece * part, part)
        return pltpu.make_async_copy(
            train_hbm.at[layer, :, columns], x.at[layer, :, columns], load_sem.at[layer, piece]
        )

    def remote(src, dst, send, recv, target):
        return pltpu.make_async_remote_copy(
            src_ref=src, dst_ref=dst, send_sem=send, recv_sem=recv,
            device_id={"ex": target}, device_id_type=pl.DeviceIdType.MESH,
        )

    for layer in range(layers):
        for piece in range(PARTS):
            load(layer, piece).start()

    barrier = pltpu.get_barrier_semaphore()

    def greet(offset):
        pl.semaphore_signal(
            barrier, inc=1, device_id={"ex": lax.rem(me + offset + 1, n)},
            device_id_type=pl.DeviceIdType.MESH,
        )

    loop(n - 1, greet, spread_out)
    gathered[me] = jnp.concatenate(
        [test_ref[layer].astype(jnp.float32) for layer in range(layers)], axis=0
    ).astype(jnp.bfloat16)
    pl.semaphore_wait(barrier, n - 1)

    groups = n // 4
    mine_a, mine_r = me // 4, me % 4
    mine_b, mine_c = mine_r // 2, mine_r % 2
    across = mine_a * 4 + (1 - mine_b) * 2 + mine_c
    beside = mine_a * 4 + mine_b * 2 + (1 - mine_c)

    def pass_on(slot, target, index):
        return remote(gathered.at[slot], gathered.at[slot], gsend.at[index], grecv.at[slot], target)

    def first(offset):
        pass_on(me, lax.rem(mine_a + offset + 1, groups) * 4 + mine_r, offset).start()

    loop(groups - 1, first)
    pass_on(me, across, groups - 1).start()
    pass_on(me, beside, 2 * groups - 1).start()

    def forward_across():
        def step(offset):
            slot = lax.rem(mine_a + groups - offset - 1, groups) * 4 + mine_r
            pass_on(slot, across, groups + offset).wait_recv()
            pass_on(slot, across, groups + offset).start()

        loop(groups - 1, step)

    def forward_beside():
        def own(offset):
            slot = lax.rem(mine_a + groups - offset - 1, groups) * 4 + mine_r
            pass_on(slot, beside, 2 * groups + offset).start()

        loop(groups - 1, own)

        def other(offset):
            slot = lax.rem(mine_a + groups - offset, groups) * 4 + (1 - mine_b) * 2 + mine_c
            pass_on(slot, beside, 3 * groups - 1 + offset).wait_recv()
            pass_on(slot, beside, 3 * groups - 1 + offset).start()

        loop(groups, other)

    def outer_stats(layer):
        acc_out[...] = jnp.zeros_like(acc_out)
        for piece in range(PARTS):
            load(layer, piece).wait()

            def step(index, piece=piece):
                start = pl.multiple_of(piece * part + index * WIDE, WIDE)
                block = x[layer, :, pl.ds(start, WIDE)]
                turned = block.T
                acc_out[...] += dot(turned, block)
                first_block = piece * (part // K) + index * (WIDE // K)
                for r in range(row_blocks):
                    for u in range(WIDE // K):
                        xt[pl.ds((r * K + first_block + u) * PITCH, K), :] = turned[
                            u * K : (u + 1) * K, r * LANES : (r + 1) * LANES
                        ].astype(jnp.float32)

            loop(part // WIDE, step, 4)

    def inner_stats(layer):
        acc_in[...] = jnp.zeros_like(acc_in)

        def step(index):
            block = jnp.concatenate(
                [
                    jnp.concatenate(
                        [
                            xt[pl.ds(r * K * PITCH + index * 4 + u, K, stride=PITCH), :].astype(jnp.bfloat16)
                            for r in range(row_blocks)
                        ],
                        axis=1,
                    )
                    for u in range(4)
                ],
                axis=0,
            )
            acc_in[...] += dot(block, block, ((1,), (1,)))

        loop(K // 4, step, 4)

    lane = lax.broadcasted_iota(jnp.int32, (K, LANES), 1)
    sub = lax.broadcasted_iota(jnp.int32, (K, LANES), 0)
    low_half = lane < K

    for layer in range(layers):
        outer_stats(layer)
        inner_stats(layer)
        if layer == 0:
            forward_across()
        stats[layer * K : (layer + 1) * K, :] = jnp.where(
            low_half, fold(acc_in[...])[0], fold(acc_out[...])[1]
        )

    def tile_rows(owner):
        return pl.ds(pl.multiple_of(owner * tile, tile), tile)

    def to_owner(owner):
        return remote(stats.at[tile_rows(owner)], reduce_buf.at[me], rsend.at[owner], rrecv.at[me], owner)

    def only(condition, action):
        if owners == n:
            action()
        else:
            pl.when(condition)(action)

    def send_tile(offset):
        owner = lax.rem(me + offset + 1, n)
        only(owner < owners, lambda: to_owner(owner).start())

    loop(n - 1, send_tile, spread_out)
    def from_owner(owner, target, index):
        return remote(reduced.at[tile_rows(owner)], reduced.at[tile_rows(owner)], asend.at[index], arecv.at[owner], target)

    def reduce_own():
        reduce_buf[me] = stats[tile_rows(me), :]

        def arrive(offset):
            source = lax.rem(me + n - offset - 1, n)
            remote(reduce_buf.at[source], reduce_buf.at[source], rsend.at[0], rrecv.at[source], source).wait_recv()

        loop(n - 1, arrive, spread_out)
        total = reduce_buf[0]
        for source in range(1, n):
            total = total + reduce_buf[source]
        reduced[tile_rows(me), :] = total / total_rows

        def spread(offset):
            from_owner(me, lax.rem(me + offset + 1, n), offset).start()

        loop(n - 1, spread, spread_out)

    only(me < owners, reduce_own)
    forward_beside()

    def arrive_total(offset):
        owner = lax.rem(me + n - offset - 1, n)
        only(owner < owners, lambda: from_owner(owner, owner, 0).wait_recv())

    loop(n - 1, arrive_total, spread_out)

    states = []
    for layer in range(layers):
        value = reduced[layer * K : (layer + 1) * K, :]
        diagonal = (lane == sub) | (lane == sub + K)
        on = jnp.where(diagonal, value, 0.0)
        trace_in = jnp.sum(jnp.where(low_half, on, 0.0))
        trace_out = jnp.sum(jnp.where(low_half, 0.0, on))
        damping = 0.1 * jnp.where(low_half, trace_in, trace_out) / K
        states.append(jnp.where(diagonal, value + damping, value))

    for k in range(K):
        place = jnp.where(low_half, k, k + K)
        at_column, at_row = lane == place, sub == k
        for layer in range(layers):
            value = states[layer]
            row = value[k : k + 1]
            column = jnp.take_along_axis(value, place, axis=1, mode="promise_in_bounds")
            pivot = jnp.take_along_axis(
                jnp.broadcast_to(row, (8, LANES)), place[:8], axis=1, mode="promise_in_bounds"
            )
            inverse = 1.0 / pivot[:1]
            scaled = row * inverse
            new = jnp.where(at_column, column * inverse, value - column * scaled)
            states[layer] = jnp.where(at_row, jnp.where(at_column, -inverse, scaled), new)

    def arrive_beside(offset):
        slot = offset * 2 + (1 - mine_c)
        pass_on(slot, beside, 0).wait_recv()

    loop(n // 2, arrive_beside)

    per_block = LANES // 8

    def turn_queries(index):
        start = pl.multiple_of(index * LANES, LANES)
        for block in range(query_blocks):
            values = gathered[block * per_block : (block + 1) * per_block, :, pl.ds(start, LANES)].astype(jnp.float32)
            for layer in range(layers):
                turned = values[:, layer * 8 : (layer + 1) * 8, :].reshape(LANES, LANES).T
                queries[layer, block, pl.ds(start, LANES), :] = turned.astype(jnp.bfloat16)

    loop(FEATURES // LANES, turn_queries, 4)

    scores[...] = jnp.zeros_like(scores)
    for layer in range(layers):
        inverse = -states[layer]
        high = inverse.astype(jnp.bfloat16).astype(jnp.float32)
        rest = inverse - high
        right_pair = jnp.where(low_half, pltpu.roll(high, K, 1), rest).astype(jnp.bfloat16)
        left_pair = jnp.where(low_half, high, pltpu.roll(rest, K, 1)).astype(jnp.bfloat16)
        left_four = jnp.concatenate([left_pair, left_pair], axis=1)
        for block in range(query_blocks):

            def apply_right(index, layer=layer, block=block):
                start = pl.multiple_of(index * 4 * K, 4 * K)
                wide = [queries[layer, block, pl.ds(start + u * K, K), :] for u in range(4)]
                wide = jnp.concatenate(wide, axis=1)
                result = dot(right_pair, jnp.concatenate([wide, wide], axis=0))
                for u in range(4):
                    right[pl.ds((index * 4 + u) * PITCH, K), :] = result[:, u * LANES : (u + 1) * LANES]

            loop(K // 4, apply_right, 8)

            def apply_left(index):
                value = jnp.concatenate(
                    [right[pl.ds(index * 4 + u, K, stride=PITCH), :] for u in range(4)], axis=1
                )
                upper = value.astype(jnp.bfloat16)
                lower = (value - upper.astype(jnp.float32)).astype(jnp.bfloat16)
                result = dot(left_four, jnp.concatenate([upper, upper, lower, lower], axis=0))
                for u in range(4):
                    both[pl.ds(index * 4 + u, K, stride=PITCH), :] = result[:, u * LANES : (u + 1) * LANES]

            loop(K // 4, apply_left, 8)

            def score(index, layer=layer, block=block):
                start = pl.multiple_of(index * 1024, 1024)
                weights = [
                    both[pl.ds((index * 16 + u) * PITCH, K), :].astype(jnp.bfloat16) for u in range(16)
                ]
                scores[block] += dot(x[layer, :, pl.ds(start, 1024)], jnp.concatenate(weights, axis=0))

            loop(FEATURES // 1024, score)

    for block in range(query_blocks):
        value = scores[block]
        power_buf[me, :, block * LANES : (block + 1) * LANES] = jnp.broadcast_to(
            jnp.sum(value * value, axis=0, keepdims=True), (8, LANES)
        )

    def send_power(offset):
        target = lax.rem(me + offset + 1, n)
        remote(power_buf.at[me], power_buf.at[me], psend.at[offset], precv.at[me], target).start()

    loop(n - 1, send_power, spread_out)

    def arrive_power(offset):
        source = lax.rem(me + n - offset - 1, n)
        remote(power_buf.at[source], power_buf.at[source], psend.at[0], precv.at[source], source).wait_recv()

    loop(n - 1, arrive_power, spread_out)
    power = power_buf[0]
    for source in range(1, n):
        power = power + power_buf[source]
    scale = lax.rsqrt(power / total_rows + 1e-06)
    for block in range(query_blocks):
        columns = slice(block * LANES, (block + 1) * LANES)
        out_ref[:, columns] = (scores[block] * scale[:1, columns]).astype(out_ref.dtype)

    def sent_queries(index):
        pass_on(me, beside, index).wait_send()

    loop(n - 1, sent_queries, spread_out)

    def sent_tile(offset):
        owner = lax.rem(me + offset + 1, n)
        only(owner < owners, lambda: to_owner(owner).wait_send())

    loop(n - 1, sent_tile, spread_out)

    def sent_total():
        loop(n - 1, lambda offset: from_owner(me, beside, offset).wait_send(), spread_out)

    only(me < owners, sent_total)

    def sent_power(offset):
        remote(power_buf.at[me], power_buf.at[me], psend.at[offset], precv.at[me], beside).wait_send()

    loop(n - 1, sent_power, spread_out)


def body(train_features, test_features):
    layers, rows, features = train_features.shape
    count = test_features.shape[1]
    n = lax.axis_size("ex")
    query_count = count * n
    query_blocks = query_count // LANES
    owners = min(n, TILES)
    f32, bf16 = jnp.float32, jnp.bfloat16
    dma = pltpu.SemaphoreType.DMA
    return pl.pallas_call(
        functools.partial(kernel, n, rows * n),
        out_shape=jax.ShapeDtypeStruct((rows, query_count), bf16),
        in_specs=[pl.BlockSpec(memory_space=pl.ANY), pl.BlockSpec(memory_space=pltpu.VMEM)],
        out_specs=pl.BlockSpec(memory_space=pltpu.VMEM),
        scratch_shapes=[
            pltpu.VMEM((layers, rows, features), bf16),
            pltpu.VMEM((rows // LANES * K * PITCH, LANES), f32),
            pltpu.VMEM((WIDE, WIDE), f32),
            pltpu.VMEM((WIDE, WIDE), f32),
            pltpu.VMEM((n, layers * count, features), bf16),
            pltpu.VMEM((layers, query_blocks, features, LANES), bf16),
            pltpu.VMEM((K * PITCH, LANES), f32),
            pltpu.VMEM((K * PITCH, LANES), f32),
            pltpu.VMEM((query_blocks, rows, LANES), f32),
            pltpu.VMEM((layers * K, LANES), f32),
            pltpu.VMEM((n, layers * K // owners, LANES), f32),
            pltpu.VMEM((layers * K, LANES), f32),
            pltpu.VMEM((n, 8, query_count), f32),
            dma((layers, PARTS)),
            dma((n,)), dma((n,)), dma((n,)), dma((n,)),
            dma((n,)), dma((n,)), dma((n,)), dma((n,)),
        ],
        compiler_params=pltpu.CompilerParams(
            collective_id=0, has_side_effects=True, vmem_limit_bytes=60 * 1024 * 1024
        ),
    )(train_features, test_features)


def solution(mesh):
    in_specs = (P(None, ("grp", "ex"), None), P(None, ("grp", "ex"), None))
    out_specs = P(("grp", "ex"), None)
    return jax.shard_map(body, mesh=mesh, in_specs=in_specs, out_specs=out_specs, check_vma=False)
```
